128 devices in a mesh: span: 8 (over y_hi, z), seq: 16 (over x, y_lo, core).
Axes of the slice: x: 4, y: 4 (y_hi: 2, y_lo: 2; y = y_hi * 2 + y_lo), z: 4, core: 2. Of those that a mesh axis runs over, the one named last changes fastest.
Arguments:
- queries: bfloat16 [8, 512, 4096], P('span', 'seq')
- keys: bfloat16 [8, 512, 4096], P('span', 'seq')
- values: bfloat16 [8, 512, 4096], P('span', 'seq'), may hold values from -6 to 6
- gate_table: float32 [50, 4096], replicated, may hold values from -6 to 6
- levels: int32 [8], replicated, may hold values from 0 to 49
- span_rank: int32 [8], replicated, may hold values from 0 to 7, each once
Outputs:
- gated: bfloat16 [8, 512, 4096], P('span', 'seq')
The draws below stay inside these ranges and needn't reach their ends.
Inputs may be any that keep to these rules, and one draw needn't show every extreme that they name: `span_rank`: each span has one place in time, each place used once.
All inputs are finite; a program needn't handle non-finite values.
Results may differ from the reference program's by a relative error of at most 0.012.
Values may be sent and summed in bfloat16 or wider, within the bound.
No kernel may reach another device: no remote copies, remote signals or barrier semaphores. Data moves between devices by JAX's collectives and lax.ppermute only.
A program may use at most 192 MiB of HBM per device.

```python
import jax
import jax.numpy as jnp
from jax import lax

HEADS = 32
HD = 128
LEVELS = 50
SPAN_LEN = 512
SPANS = 8
WIDTH = 4096


def shared_keys(key):
    width = HEADS * HD
    base = jax.random.normal(jax.random.fold_in(key, 11), (SPANS, SPAN_LEN, width), jnp.float32)
    rows = jnp.arange(SPAN_LEN) % 61 == 8
    near = base
    return jnp.where(rows[None, :, None], near, base)


def draw_keys(key, part):
    return shared_keys(key).astype(jnp.bfloat16)


def draw_queries(key, part):
    width = HEADS * HD
    key = jax.random.fold_in(key, 5)
    return jax.random.normal(key, (SPANS, SPAN_LEN, width), jnp.float32).astype(jnp.bfloat16)


def with_ends(drawn, key, least, largest):
    longest = drawn.shape.index(max(drawn.shape))
    spots = []
    for shift in (0, 1):
        where = [jax.random.randint(jax.random.fold_in(key, axis), (), 0, length) for axis, length in enumerate(drawn.shape)]
        where[longest] = (where[longest] + shift) % drawn.shape[longest]
        spots.append(tuple(where))
    return drawn.at[spots[0]].set(least).at[spots[1]].set(largest)


def block_levels(own_key, extent, shards, low, top_value):
    gain, own = 1.0, jax.random.fold_in(own_key, 6)
    for dim, shards_of in shards:
        draws = jnp.exp(jax.random.uniform(jax.random.fold_in(own, dim), (shards_of,), jnp.float32, low / len(shards), top_value / len(shards)))
        gain = gain * jnp.repeat(draws, extent[dim] // shards_of).reshape([-1 if axis == dim else 1 for axis in range(len(extent))])
    return gain


def scatter_about(rng, extent, scale, most, cuts=(), held_as=jnp.bfloat16):
    values = scale * jax.random.normal(rng, extent, jnp.float32)
    if cuts:
        values = values * block_levels(rng, extent, cuts, -0.22, 0.18)
    return jnp.clip(values, -most, most).astype(held_as)


def setup_inputs(seed: int = 0) -> dict:
    seeds = jax.random.split(jax.random.key(seed), 7)
    queries = draw_queries(jax.random.fold_in(seeds[6], 71), 0)
    keys = draw_keys(jax.random.fold_in(seeds[6], 71), 0)
    values = scatter_about(seeds[2], (SPANS, SPAN_LEN, WIDTH), 1.0, 6.0, ((0, 8), (1, 16)))
    gate_table = scatter_about(seeds[3], (LEVELS, WIDTH), 1.0, 6.0, (), jnp.float32)
    levels = with_ends(jax.random.randint(seeds[4], (SPANS,), 0, LEVELS), jax.random.fold_in(seeds[4], 1), 0, LEVELS - 1).astype(jnp.int32)
    span_rank = jax.random.permutation(seeds[5], SPANS).astype(jnp.int32)
    return dict(queries=queries, keys=keys, values=values, gate_table=gate_table, levels=levels, span_rank=span_rank)


def reference(queries, keys, values, gate_table, levels, span_rank):
    width = HEADS * HD
    score_scale = 1.0 / (HD ** 0.5)
    key_heads = keys.reshape(SPANS * SPAN_LEN, HEADS, HD).transpose(1, 0, 2)
    value_heads = values.reshape(SPANS * SPAN_LEN, HEADS, HD).transpose(1, 0, 2)
    key_rank = jnp.repeat(span_rank, SPAN_LEN)
    results = []
    for which in range(SPANS):
        visible = key_rank <= span_rank[which]
        query_heads = queries[which].reshape(SPAN_LEN, HEADS, HD).transpose(1, 0, 2)

        def one_head(operands):
            query_h, key_h, value_h = operands
            scores = jnp.dot(query_h, key_h.T, preferred_element_type=jnp.float32) * score_scale
            masked = jnp.where(visible[None, :], scores, -1e30)
            top = jnp.max(masked, axis=1, keepdims=True)
            expo = jnp.where(visible[None, :], jnp.exp(masked - top), 0.0)
            total = jnp.sum(expo, axis=1, keepdims=True)
            numer = jnp.dot(expo.astype(jnp.bfloat16), value_h, preferred_element_type=jnp.float32)
            return numer / total

        attended = lax.map(one_head, (query_heads, key_heads, value_heads))
        attended = attended.transpose(1, 0, 2).reshape(SPAN_LEN, width).astype(jnp.bfloat16)
        gate_row = gate_table[levels[which]]
        results.append((gate_row[None, :] * attended.astype(jnp.float32)).astype(jnp.bfloat16))
    return jnp.stack(results, axis=0)
```

```python
import functools

import jax
import jax.numpy as jnp
from jax import lax
from jax.experimental import pallas as pl
from jax.experimental.pallas import tpu as pltpu
from jax.sharding import Mesh
from jax.sharding import PartitionSpec as P

HD = 128
AXES = ("yh", "z", "x", "yl", "c")
SIZES = (2, 4, 4, 2, 2)
WIDE = ("yh", "z", "x")
NEAR = ("yl", "c")
MIB = 1 << 20


def pack_body(q_ref, k_ref, v_ref, o_ref):
    heads, rows3, hd = o_ref.shape
    rows = rows3 // 3
    for h in range(heads):
        cols = slice(h * hd, (h + 1) * hd)
        o_ref[h, 0:rows, :] = q_ref[:, cols]
        o_ref[h, rows : 2 * rows, :] = k_ref[:, cols]
        o_ref[h, 2 * rows :, :] = v_ref[:, cols]


def pack(q, k, v):
    rows, width = q.shape
    return pl.pallas_call(
        pack_body,
        out_shape=jax.ShapeDtypeStruct((width // HD, 3 * rows, HD), q.dtype),
        in_specs=[pl.BlockSpec(memory_space=pltpu.VMEM)] * 3,
        out_specs=pl.BlockSpec(memory_space=pltpu.VMEM),
        name="pack",
    )(q, k, v)


def attend_body(order, q_ref, kv_ref, o_ref, q_s, k_s, v_s):
    near, spans, xs, rows2, hd = kv_ref.shape
    rows = rows2 // 2
    q_rows = xs * rows
    k_rows = near * q_rows
    factor = 1.4426950408889634 / hd**0.5
    for r in range(spans):
        span = order[r]
        for i in range(xs):
            q_s[pl.ds(r * q_rows + i * rows, rows), :] = q_ref[span, i, 0:rows, :]
            for n in range(near):
                at = pl.ds(r * k_rows + (n * xs + i) * rows, rows)
                k_s[at, :] = kv_ref[n, span, i, 0:rows, :]
                v_s[at, :] = kv_ref[n, span, i, rows:, :]
    for r in range(spans):
        seen = (r + 1) * k_rows
        q = q_s[r * q_rows : (r + 1) * q_rows, :]
        s = lax.dot_general(
            q, k_s[0:seen, :], (((1,), (1,)), ((), ())), preferred_element_type=jnp.float32
        )
        top = jnp.max(s, axis=1, keepdims=True)
        e = jnp.exp2((s - top) * factor)
        total = jnp.sum(e, axis=1, keepdims=True)
        acc = jnp.dot(e.astype(jnp.bfloat16), v_s[0:seen, :], preferred_element_type=jnp.float32)
        out = (acc / total).astype(o_ref.dtype)
        span = order[r]
        for i in range(xs):
            o_ref[span, i] = out[i * rows : (i + 1) * rows, :]


def attend(order, q, kv):
    near, spans, xs, rows2, hd = kv.shape
    rows = rows2 // 2
    q_total = spans * xs * rows
    vmem = pl.BlockSpec(memory_space=pltpu.VMEM)
    return pl.pallas_call(
        attend_body,
        out_shape=jax.ShapeDtypeStruct((spans, xs, rows, hd), q.dtype),
        in_specs=[pl.BlockSpec(memory_space=pltpu.SMEM), vmem, vmem],
        out_specs=vmem,
        scratch_shapes=[
            pltpu.VMEM((q_total, hd), q.dtype),
            pltpu.VMEM((near * q_total, hd), q.dtype),
            pltpu.VMEM((near * q_total, hd), q.dtype),
        ],
        compiler_params=pltpu.CompilerParams(vmem_limit_bytes=40 * MIB),
        name="attend",
    )(order, q, kv)


def finish_body(level, a_ref, g_ref, o_ref):
    heads, rows, hd = a_ref.shape
    gate = g_ref[pl.ds(level[0], 1), :]
    for h in range(heads):
        cols = slice(h * hd, (h + 1) * hd)
        o_ref[:, cols] = (gate[:, cols] * a_ref[h].astype(jnp.float32)).astype(o_ref.dtype)


def finish(level, attended, gate_table):
    heads, rows, hd = attended.shape
    vmem = pl.BlockSpec(memory_space=pltpu.VMEM)
    return pl.pallas_call(
        finish_body,
        out_shape=jax.ShapeDtypeStruct((rows, heads * hd), attended.dtype),
        in_specs=[pl.BlockSpec(memory_space=pltpu.SMEM), vmem, vmem],
        out_specs=vmem,
        name="finish",
    )(level, attended, gate_table)


def local(queries, keys, values, gate_table, levels, span_rank):
    spans = span_rank.shape[0]
    places = jnp.arange(spans, dtype=jnp.int32)
    order = jnp.sum(
        jnp.where(span_rank[None, :] == places[:, None], places[None, :], 0), axis=1
    ).astype(jnp.int32)
    my_span = lax.axis_index(("yh", "z"))
    level = jnp.sum(jnp.where(places == my_span, levels, 0)).reshape(1)
    packed = pack(queries[0], keys[0], values[0])
    mine = lax.all_to_all(packed, WIDE, 0, 0, tiled=True)
    rows = queries.shape[1]
    kv = lax.all_gather(mine[:, rows:, :], NEAR, axis=0, tiled=False)
    xs = SIZES[2]
    q = mine.reshape(spans, xs, 3 * rows, HD)
    out = attend(order, q, kv.reshape(kv.shape[0], spans, xs, 2 * rows, HD))
    back = lax.all_to_all(out.reshape(spans * xs, rows, HD), WIDE, 0, 0, tiled=True)
    return finish(level, back, gate_table)[None]


def solution(mesh):
    fine = Mesh(mesh.devices.reshape(SIZES), AXES)
    split = P(("yh", "z"), ("x", "yl", "c"), None)
    return jax.shard_map(
        local,
        mesh=fine,
        in_specs=(split, split, split, P(), P(), P()),
        out_specs=split,
        check_vma=False,
    )
```

```python
import jax
import jax.numpy as jnp
from jax import lax
from jax.experimental import pallas as pl
from jax.experimental.pallas import tpu as pltpu
from jax.sharding import Mesh
from jax.sharding import PartitionSpec as P

HD = 128
AXES = ("yh", "z", "x", "yl", "c")
SIZES = (2, 4, 4, 2, 2)
HEAD_AXES = ("yh", "z", "x")
WIDE = ("yh", "z", "x", "yl")
MIB = 1 << 20
VMEM_WHOLE = pl.BlockSpec(memory_space=pltpu.VMEM)
SMEM_WHOLE = pl.BlockSpec(memory_space=pltpu.SMEM)


def pack_body(q_ref, k_ref, v_ref, o_ref):
    rows, width = q_ref.shape
    heads = width // HD
    parts = o_ref.shape[0] // heads
    q_rows = rows // parts
    for h in range(heads):
        cols = slice(h * HD, (h + 1) * HD)
        for p in range(parts):
            to = h * parts + p
            o_ref[to, 0:q_rows, :] = q_ref[p * q_rows : (p + 1) * q_rows, cols]
            o_ref[to, q_rows : q_rows + rows, :] = k_ref[:, cols]
            o_ref[to, q_rows + rows :, :] = v_ref[:, cols]


def pack(q, k, v, parts):
    rows, width = q.shape
    return pl.pallas_call(
        pack_body,
        out_shape=jax.ShapeDtypeStruct(
            (width // HD * parts, rows // parts + 2 * rows, HD), q.dtype
        ),
        in_specs=[VMEM_WHOLE] * 3,
        out_specs=VMEM_WHOLE,
        compiler_params=pltpu.CompilerParams(vmem_limit_bytes=6 * MIB),
        name="pack",
    )(q, k, v)


def attend_body(rank, levels, head, near_ref, far_ref, gate_ref, o_ref, q_s, k_s, v_s, g_s, sem):
    spans, senders, packed, hd = near_ref.shape
    q_rows = o_ref.shape[2]
    rows = (packed - q_rows) // 2
    q_step = senders * q_rows
    k_step = 2 * senders * rows
    factor = 1.4426950408889634 / hd**0.5
    columns = pl.ds(pl.multiple_of(head[0] * hd, hd), hd)
    fetch = pltpu.make_async_copy(gate_ref.at[:, columns], g_s, sem)
    fetch.start()
    for span in range(spans):
        r = rank[span]
        q_at = pl.multiple_of(r * q_step, q_step)
        k_at = pl.multiple_of(r * k_step, k_step)
        for i in range(senders):
            q_s[pl.ds(q_at + i * q_rows, q_rows), :] = near_ref[span, i, 0:q_rows, :]
            for n, ref in enumerate((near_ref, far_ref)):
                at = pl.ds(k_at + (n * senders + i) * rows, rows)
                k_s[at, :] = ref[span, i, q_rows : q_rows + rows, :]
                v_s[at, :] = ref[span, i, q_rows + rows :, :]
    fetch.wait()
    for r in range(spans):
        span = jnp.int32(0)
        for place in range(1, spans):
            span = jnp.where(rank[place] == r, place, span)
        seen = (r + 1) * k_step
        s = lax.dot_general(
            q_s[r * q_step : (r + 1) * q_step, :],
            k_s[0:seen, :],
            (((1,), (1,)), ((), ())),
            preferred_element_type=jnp.float32,
        )
        top = jnp.max(s, axis=1, keepdims=True)
        e = jnp.exp2((s - top) * factor)
        total = jnp.sum(e, axis=1, keepdims=True)
        acc = jnp.dot(e.astype(jnp.bfloat16), v_s[0:seen, :], preferred_element_type=jnp.float32)
        attended = (acc / total).astype(jnp.bfloat16).astype(jnp.float32)
        gated = (g_s[pl.ds(levels[span], 1), :] * attended).astype(o_ref.dtype)
        for i in range(senders):
            o_ref[span, i] = gated[i * q_rows : (i + 1) * q_rows, :]


def attend(rank, levels, head, near, far, gate_table, q_rows):
    spans, senders, packed, hd = near.shape
    rows = (packed - q_rows) // 2
    q_total = spans * senders * q_rows
    k_total = 2 * spans * senders * rows
    return pl.pallas_call(
        attend_body,
        out_shape=jax.ShapeDtypeStruct((spans, senders, q_rows, hd), near.dtype),
        in_specs=[
            SMEM_WHOLE,
            SMEM_WHOLE,
            SMEM_WHOLE,
            VMEM_WHOLE,
            VMEM_WHOLE,
            pl.BlockSpec(memory_space=pl.ANY),
        ],
        out_specs=VMEM_WHOLE,
        scratch_shapes=[
            pltpu.VMEM((q_total, hd), near.dtype),
            pltpu.VMEM((k_total, hd), near.dtype),
            pltpu.VMEM((k_total, hd), near.dtype),
            pltpu.VMEM((gate_table.shape[0], hd), gate_table.dtype),
            pltpu.SemaphoreType.DMA,
        ],
        compiler_params=pltpu.CompilerParams(vmem_limit_bytes=24 * MIB),
        name="attend",
    )(rank, levels, head, near, far, gate_table)


def unpack_body(a_ref, o_ref):
    parts_heads, q_rows, hd = a_ref.shape
    parts = o_ref.shape[0] // q_rows
    for h in range(parts_heads // parts):
        for p in range(parts):
            o_ref[p * q_rows : (p + 1) * q_rows, h * hd : (h + 1) * hd] = a_ref[h * parts + p]


def unpack(a, rows):
    parts_heads, q_rows, hd = a.shape
    return pl.pallas_call(
        unpack_body,
        out_shape=jax.ShapeDtypeStruct((rows, parts_heads * q_rows // rows * hd), a.dtype),
        in_specs=[VMEM_WHOLE],
        out_specs=VMEM_WHOLE,
        compiler_params=pltpu.CompilerParams(vmem_limit_bytes=4 * MIB),
        name="unpack",
    )(a)


def local(queries, keys, values, gate_table, levels, span_rank):
    spans = span_rank.shape[0]
    rows = queries.shape[1]
    parts = SIZES[3]
    q_rows = rows // parts
    head = lax.axis_index(HEAD_AXES).astype(jnp.int32).reshape(1)
    packed = pack(queries[0], keys[0], values[0], parts)
    near = lax.all_to_all(packed, WIDE, 0, 0, tiled=True)
    far = lax.ppermute(near, "c", [(0, 1), (1, 0)])
    senders = near.shape[0] // spans
    shape = (spans, senders) + near.shape[1:]
    out = attend(
        span_rank, levels, head, near.reshape(shape), far.reshape(shape), gate_table, q_rows
    )
    back = lax.all_to_all(out.reshape(spans * senders, q_rows, HD), WIDE, 0, 0, tiled=True)
    return unpack(back, rows)[None]


def solution(mesh):
    fine = Mesh(mesh.devices.reshape(SIZES), AXES)
    split = P(("yh", "z"), ("x", "yl", "c"), None)
    return jax.shard_map(
        local,
        mesh=fine,
        in_specs=(split, split, split, P(), P(), P()),
        out_specs=split,
        check_vma=False,
    )
```

```python
import jax
import jax.numpy as jnp
from jax import lax
from jax.experimental import pallas as pl
from jax.experimental.pallas import tpu as pltpu
from jax.sharding import Mesh
from jax.sharding import PartitionSpec as P

HD = 128
AXES = ("yh", "z", "x", "yl", "c")
SIZES = (2, 4, 4, 2, 2)
HEAD_AXES = ("yh", "z", "x")
WIDE = ("yh", "z", "x", "yl")
LOG2E = 1.4426950408889634
STAT = 8
MIB = 1 << 20
VMEM_WHOLE = pl.BlockSpec(memory_space=pltpu.VMEM)
SMEM_WHOLE = pl.BlockSpec(memory_space=pltpu.SMEM)
ANYWHERE = pl.BlockSpec(memory_space=pl.ANY)


def pack_body(q_any, k_any, v_any, o_ref, q_ref, k_ref, v_ref, sems):
    copies = [
        pltpu.make_async_copy(src, dst, sems.at[i])
        for i, (src, dst) in enumerate(((q_any, q_ref), (k_any, k_ref), (v_any, v_ref)))
    ]
    for copy in copies:
        copy.start()
    rows, width = q_ref.shape
    heads = width // HD
    parts = o_ref.shape[0] // heads
    k_rows = rows // parts
    copies[0].wait()
    for h in range(heads):
        block = q_ref[:, h * HD : (h + 1) * HD]
        for p in range(parts):
            o_ref[h * parts + p, 0:rows, :] = block
    for n, ref in enumerate((k_ref, v_ref)):
        copies[n + 1].wait()
        for h in range(heads):
            for p in range(parts):
                o_ref[h * parts + p, rows + n * k_rows : rows + (n + 1) * k_rows, :] = ref[
                    p * k_rows : (p + 1) * k_rows, h * HD : (h + 1) * HD
                ]


def pack(q, k, v, parts):
    rows, width = q.shape
    return pl.pallas_call(
        pack_body,
        out_shape=jax.ShapeDtypeStruct(
            (width // HD * parts, rows + 2 * (rows // parts), HD), q.dtype
        ),
        in_specs=[ANYWHERE] * 3,
        out_specs=VMEM_WHOLE,
        scratch_shapes=[pltpu.VMEM((rows, width), q.dtype)] * 3
        + [pltpu.SemaphoreType.DMA((3,))],
        compiler_params=pltpu.CompilerParams(vmem_limit_bytes=6 * MIB),
        name="pack",
    )(q, k, v)


def attend_body(rank, levels, head, near_ref, far_ref, gate_ref, o_ref, q_s, k_s, v_s, g_s, sem):
    spans, senders, packed, hd = near_ref.shape
    rows = o_ref.shape[2] - STAT
    k_rows = (packed - rows) // 2
    q_step = senders * rows
    k_step = 2 * senders * k_rows
    factor = LOG2E / hd**0.5
    columns = pl.ds(pl.multiple_of(head[0] * hd, hd), hd)
    fetch = pltpu.make_async_copy(gate_ref.at[:, columns], g_s, sem)
    fetch.start()
    for span in range(spans):
        r = rank[span]
        q_at = pl.multiple_of(r * q_step, q_step)
        k_at = pl.multiple_of(r * k_step, k_step)
        for i in range(senders):
            q_s[pl.ds(q_at + i * rows, rows), :] = near_ref[span, i, 0:rows, :]
            for n, ref in enumerate((near_ref, far_ref)):
                at = pl.ds(k_at + (n * senders + i) * k_rows, k_rows)
                k_s[at, :] = ref[span, i, rows : rows + k_rows, :]
                v_s[at, :] = ref[span, i, rows + k_rows :, :]
    fetch.wait()
    diagonal = lax.broadcasted_iota(jnp.int32, (hd, hd), 0) == lax.broadcasted_iota(
        jnp.int32, (hd, hd), 1
    )
    for r in range(spans):
        span = jnp.int32(0)
        for place in range(1, spans):
            span = jnp.where(rank[place] == r, place, span)
        seen = (r + 1) * k_step
        s = lax.dot_general(
            q_s[r * q_step : (r + 1) * q_step, :],
            k_s[0:seen, :],
            (((1,), (1,)), ((), ())),
            preferred_element_type=jnp.float32,
        )
        top = jnp.max(s, axis=1, keepdims=True)
        e = jnp.exp2((s - top) * factor)
        total = jnp.sum(e, axis=1, keepdims=True)
        acc = jnp.dot(e.astype(jnp.bfloat16), v_s[0:seen, :], preferred_element_type=jnp.float32)
        gated = (g_s[pl.ds(levels[span], 1), :] * (acc / total)).astype(o_ref.dtype)
        logs = top * factor + jnp.log2(total)
        for i in range(senders):
            o_ref[span, i, 0:rows, :] = gated[i * rows : (i + 1) * rows, :]
        for j in range(q_step // hd):
            line = jnp.sum(
                jnp.where(diagonal, logs[j * hd : (j + 1) * hd, :], 0.0), axis=0, keepdims=True
            )
            high = line.astype(jnp.bfloat16).astype(jnp.float32)
            middle = (line - high).astype(jnp.bfloat16).astype(jnp.float32)
            low = line - high - middle
            stat = jnp.concatenate(
                [high, middle, low, jnp.zeros((STAT - 3, hd), jnp.float32)], axis=0
            ).astype(o_ref.dtype)
            for i in range(j * hd // rows, (j + 1) * hd // rows):
                o_ref[span, i, rows : rows + STAT, :] = stat


def attend(rank, levels, head, near, far, gate_table, rows):
    spans, senders, packed, hd = near.shape
    q_total = spans * senders * rows
    k_total = spans * senders * (packed - rows)
    return pl.pallas_call(
        attend_body,
        out_shape=jax.ShapeDtypeStruct((spans, senders, rows + STAT, hd), near.dtype),
        in_specs=[SMEM_WHOLE, SMEM_WHOLE, SMEM_WHOLE, VMEM_WHOLE, VMEM_WHOLE, ANYWHERE],
        out_specs=VMEM_WHOLE,
        scratch_shapes=[
            pltpu.VMEM((q_total, hd), near.dtype),
            pltpu.VMEM((k_total, hd), near.dtype),
            pltpu.VMEM((k_total, hd), near.dtype),
            pltpu.VMEM((gate_table.shape[0], hd), gate_table.dtype),
            pltpu.SemaphoreType.DMA,
        ],
        compiler_params=pltpu.CompilerParams(vmem_limit_bytes=24 * MIB),
        name="attend",
    )(rank, levels, head, near, far, gate_table)


def join_body(place, a_ref, o_ref, w_s):
    heads, _, packed, hd = a_ref.shape
    rows = packed - STAT
    logs = [
        jnp.sum(a_ref[:, p, rows:packed, :].astype(jnp.float32), axis=1) for p in range(2)
    ]
    share = 1.0 / (1.0 + jnp.exp2(logs[1] - logs[0]))
    w_s[...] = share.T
    mine = w_s[pl.ds(pl.multiple_of(place[0] * rows, rows), rows), :]
    for h in range(heads):
        first = a_ref[h, 0, 0:rows, :].astype(jnp.float32)
        second = a_ref[h, 1, 0:rows, :].astype(jnp.float32)
        w = mine[:, h : h + 1]
        joined = w * first + (1.0 - w) * second
        o_ref[:, h * hd : (h + 1) * hd] = joined.astype(o_ref.dtype)


def join(place, a):
    heads, _, packed, hd = a.shape
    return pl.pallas_call(
        join_body,
        out_shape=jax.ShapeDtypeStruct((packed - STAT, heads * hd), a.dtype),
        in_specs=[SMEM_WHOLE, VMEM_WHOLE],
        out_specs=VMEM_WHOLE,
        scratch_shapes=[pltpu.VMEM((hd, heads), jnp.float32)],
        compiler_params=pltpu.CompilerParams(vmem_limit_bytes=4 * MIB),
        name="join",
    )(place, a)


def local(queries, keys, values, gate_table, levels, span_rank):
    spans = span_rank.shape[0]
    rows = queries.shape[1]
    parts = SIZES[3]
    head = lax.axis_index(HEAD_AXES).astype(jnp.int32).reshape(1)
    place = lax.rem(lax.axis_index(("x", "yl")), HD // rows).astype(jnp.int32).reshape(1)
    packed = pack(queries[0], keys[0], values[0], parts)
    near = lax.all_to_all(packed, WIDE, 0, 0, tiled=True)
    far = lax.ppermute(near, "c", [(0, 1), (1, 0)])
    senders = near.shape[0] // spans
    shape = (spans, senders) + near.shape[1:]
    out = attend(
        span_rank, levels, head, near.reshape(shape), far.reshape(shape), gate_table, rows
    )
    back = lax.all_to_all(
        out.reshape(spans * senders, rows + STAT, HD), WIDE, 0, 0, tiled=True
    )
    return join(place, back.reshape(-1, parts, rows + STAT, HD))[None]


def solution(mesh):
    fine = Mesh(mesh.devices.reshape(SIZES), AXES)
    split = P(("yh", "z"), ("x", "yl", "c"), None)
    return jax.shard_map(
        local,
        mesh=fine,
        in_specs=(split, split, split, P(), P(), P()),
        out_specs=split,
        check_vma=False,
    )
```

```python
import functools

import jax
import jax.numpy as jnp
from jax import lax
from jax.experimental import pallas as pl
from jax.experimental.pallas import tpu as pltpu
from jax.sharding import Mesh
from jax.sharding import PartitionSpec as P

HD = 128
AXES = ("yh", "z", "x", "yl", "c")
SIZES = (2, 4, 4, 2, 2)
HEAD_AXES = ("yh", "z", "x")
WIDE = ("yh", "z", "x", "yl")
MIB = 1 << 20
VMEM_WHOLE = pl.BlockSpec(memory_space=pltpu.VMEM)
SMEM_WHOLE = pl.BlockSpec(memory_space=pltpu.SMEM)
HBM_WHOLE = pl.BlockSpec(memory_space=pltpu.HBM)
LOG2E = 1.4426950408889634
ROW_BY_ROW = (((1,), (1,)), ((), ()))


def pack_body(q_hbm, k_hbm, v_hbm, o_ref, q_ref, k_ref, v_ref, sems):
    copies = [
        pltpu.make_async_copy(src, dst, sems.at[i])
        for i, (src, dst) in enumerate(((q_hbm, q_ref), (k_hbm, k_ref), (v_hbm, v_ref)))
    ]
    for copy in copies:
        copy.start()
    rows, width = q_ref.shape
    heads = width // HD
    parts = o_ref.shape[0] // heads
    q_rows = rows // parts
    copies[0].wait()
    for h in range(heads):
        for p in range(parts):
            o_ref[h * parts + p, 0:q_rows, :] = q_ref[
                p * q_rows : (p + 1) * q_rows, h * HD : (h + 1) * HD
            ]
    for n, ref in enumerate((k_ref, v_ref)):
        copies[n + 1].wait()
        for h in range(heads):
            block = ref[:, h * HD : (h + 1) * HD]
            for p in range(parts):
                o_ref[h * parts + p, q_rows + n * rows : q_rows + (n + 1) * rows, :] = block


def pack(q, k, v, parts):
    rows, width = q.shape
    return pl.pallas_call(
        pack_body,
        out_shape=jax.ShapeDtypeStruct(
            (width // HD * parts, rows // parts + 2 * rows, HD), q.dtype
        ),
        in_specs=[HBM_WHOLE] * 3,
        out_specs=VMEM_WHOLE,
        scratch_shapes=[pltpu.VMEM((rows, width), q.dtype)] * 3
        + [pltpu.SemaphoreType.DMA((3,))],
        compiler_params=pltpu.CompilerParams(vmem_limit_bytes=6 * MIB),
        name="pack",
    )(*(pltpu.with_memory_space_constraint(a, pltpu.HBM) for a in (q, k, v)))


def span_order(rank, spans):
    order = []
    for place in range(spans):
        span = jnp.int32(0)
        for s in range(1, spans):
            span = jnp.where(rank[s] == place, s, span)
        order.append(span)
    return order


def score_visible(order, q_ref, kv_ref, q_rows, q_s, s_s):
    spans, senders, packed, hd = kv_ref.shape
    rows = (packed - q_rows) // 2
    q_step, k_step = senders * q_rows, senders * rows
    for r in range(spans):
        q_s[r * q_step : (r + 1) * q_step, :] = q_ref[order[r], :, 0:q_rows, :].reshape(q_step, hd)
    for b in range(spans):
        k = kv_ref[order[b], :, q_rows : q_rows + rows, :].reshape(k_step, hd)
        s_s[b * q_step :, b * k_step : (b + 1) * k_step] = lax.dot_general(
            q_s[b * q_step :, :], k, ROW_BY_ROW, preferred_element_type=jnp.float32
        )


def weighted_values(order, g, group, kv_ref, q_rows, p_s):
    spans, senders, packed, hd = kv_ref.shape
    rows = (packed - q_rows) // 2
    q_step, k_step = senders * q_rows, senders * rows
    for a in range(group - 1):
        r = g * group + a
        p_s[r * q_step : (r + 1) * q_step, (r + 1) * k_step : (g + 1) * group * k_step] = jnp.zeros(
            (q_step, (group - 1 - a) * k_step), p_s.dtype
        )
    acc = None
    for b in range((g + 1) * group):
        v = kv_ref[order[b], :, q_rows + rows :, :].reshape(k_step, hd)
        part = jnp.dot(
            p_s[g * group * q_step : (g + 1) * group * q_step, b * k_step : (b + 1) * k_step],
            v,
            preferred_element_type=jnp.float32,
        )
        acc = part if acc is None else acc + part
    return acc


def near_body(q_rows, rank, near_ref, acc_ref, top_ref, total_ref, q_s, s_s, p_s):
    spans, senders, packed, hd = near_ref.shape
    q_step, k_step = senders * q_rows, senders * (packed - q_rows) // 2
    factor = LOG2E / hd**0.5
    order = span_order(rank, spans)
    score_visible(order, near_ref, near_ref, q_rows, q_s, s_s)
    for r in range(spans):
        here = slice(r * q_step, (r + 1) * q_step)
        s = s_s[here, 0 : (r + 1) * k_step]
        top = jnp.max(s, axis=1, keepdims=True)
        e = jnp.exp2((s - top) * factor)
        top_ref[here, :] = top
        total_ref[here, :] = jnp.sum(e, axis=1, keepdims=True)
        p_s[here, 0 : (r + 1) * k_step] = e.astype(p_s.dtype)
    for g in range(spans // 2):
        acc_ref[2 * g * q_step : 2 * (g + 1) * q_step, :] = weighted_values(
            order, g, 2, near_ref, q_rows, p_s
        )


def far_body(
    q_rows, rank, levels, head, near_ref, far_ref, acc_ref, top_ref, total_ref, gate_ref,
    o_ref, q_s, s_s, p_s, g_s, scale_s, total_s, sem,
):
    spans, senders, packed, hd = near_ref.shape
    q_step, k_step = senders * q_rows, senders * (packed - q_rows) // 2
    factor = LOG2E / hd**0.5
    columns = pl.ds(pl.multiple_of(head[0] * hd, hd), hd)
    fetch = pltpu.make_async_copy(gate_ref.at[:, columns], g_s, sem)
    fetch.start()
    order = span_order(rank, spans)
    score_visible(order, near_ref, far_ref, q_rows, q_s, s_s)
    for r in range(spans):
        here = slice(r * q_step, (r + 1) * q_step)
        s = s_s[here, 0 : (r + 1) * k_step]
        top = jnp.maximum(jnp.max(s, axis=1, keepdims=True), top_ref[here, :])
        e = jnp.exp2((s - top) * factor)
        scale = jnp.exp2((top_ref[here, :] - top) * factor)
        scale_s[here, :] = scale
        total_s[here, :] = total_ref[here, :] * scale + jnp.sum(e, axis=1, keepdims=True)
        p_s[here, 0 : (r + 1) * k_step] = e.astype(p_s.dtype)
    fetch.wait()
    for g in range(spans // 2):
        acc = weighted_values(order, g, 2, far_ref, q_rows, p_s)
        for a in range(2):
            r = 2 * g + a
            here = slice(r * q_step, (r + 1) * q_step)
            both = acc_ref[here, :] * scale_s[here, :] + acc[a * q_step : (a + 1) * q_step, :]
            attended = (both / total_s[here, :]).astype(jnp.bfloat16).astype(jnp.float32)
            gated = (g_s[pl.ds(levels[order[r]], 1), :] * attended).astype(o_ref.dtype)
            o_ref[order[r]] = gated.reshape(senders, q_rows, hd)


def attend_scratch(spans, senders, q_rows, rows, hd, dtype):
    q_total, k_total = spans * senders * q_rows, spans * senders * rows
    return [
        pltpu.VMEM((q_total, hd), dtype),
        pltpu.VMEM((q_total, k_total), jnp.float32),
        pltpu.VMEM((q_total, k_total), dtype),
    ]


def attend_near(rank, near, q_rows):
    spans, senders, packed, hd = near.shape
    rows = (packed - q_rows) // 2
    q_total, k_total = spans * senders * q_rows, spans * senders * rows
    return pl.pallas_call(
        functools.partial(near_body, q_rows),
        out_shape=(
            jax.ShapeDtypeStruct((q_total, hd), jnp.float32),
            jax.ShapeDtypeStruct((q_total, 1), jnp.float32),
            jax.ShapeDtypeStruct((q_total, 1), jnp.float32),
        ),
        in_specs=[SMEM_WHOLE, VMEM_WHOLE],
        out_specs=(VMEM_WHOLE,) * 3,
        scratch_shapes=attend_scratch(spans, senders, q_rows, rows, hd, near.dtype),
        compiler_params=pltpu.CompilerParams(vmem_limit_bytes=24 * MIB),
        cost_estimate=pl.CostEstimate(
            flops=4 * q_total * k_total * hd, bytes_accessed=8 * MIB, transcendentals=0
        ),
        name="attend_near",
    )(rank, near)


def attend_far(rank, levels, head, near, far, acc, top, total, gate_table, q_rows):
    spans, senders, packed, hd = near.shape
    rows = (packed - q_rows) // 2
    q_total = spans * senders * q_rows
    return pl.pallas_call(
        functools.partial(far_body, q_rows),
        out_shape=jax.ShapeDtypeStruct((spans, senders, q_rows, hd), near.dtype),
        in_specs=[SMEM_WHOLE] * 3 + [VMEM_WHOLE] * 5 + [HBM_WHOLE],
        out_specs=VMEM_WHOLE,
        scratch_shapes=attend_scratch(spans, senders, q_rows, rows, hd, near.dtype)
        + [
            pltpu.VMEM((gate_table.shape[0], hd), gate_table.dtype),
            pltpu.VMEM((q_total, 1), jnp.float32),
            pltpu.VMEM((q_total, 1), jnp.float32),
            pltpu.SemaphoreType.DMA,
        ],
        compiler_params=pltpu.CompilerParams(vmem_limit_bytes=24 * MIB),
        name="attend_far",
    )(rank, levels, head, near, far, acc, top, total, gate_table)


def unpack_body(a_ref, o_ref):
    parts_heads, q_rows, hd = a_ref.shape
    parts = o_ref.shape[0] // q_rows
    for h in range(parts_heads // parts):
        for p in range(parts):
            o_ref[p * q_rows : (p + 1) * q_rows, h * hd : (h + 1) * hd] = a_ref[h * parts + p]


def unpack(a, rows):
    parts_heads, q_rows, hd = a.shape
    return pl.pallas_call(
        unpack_body,
        out_shape=jax.ShapeDtypeStruct((rows, parts_heads * q_rows // rows * hd), a.dtype),
        in_specs=[VMEM_WHOLE],
        out_specs=VMEM_WHOLE,
        compiler_params=pltpu.CompilerParams(vmem_limit_bytes=4 * MIB),
        name="unpack",
    )(a)


def local(queries, keys, values, gate_table, levels, span_rank):
    spans = span_rank.shape[0]
    rows = queries.shape[1]
    parts = SIZES[3]
    q_rows = rows // parts
    head = lax.axis_index(HEAD_AXES).astype(jnp.int32).reshape(1)
    packed = pack(queries[0], keys[0], values[0], parts)
    near = lax.all_to_all(packed, WIDE, 0, 0, tiled=True)
    far = lax.ppermute(near, "c", [(0, 1), (1, 0)])
    senders = near.shape[0] // spans
    shape = (spans, senders) + near.shape[1:]
    near, far = near.reshape(shape), far.reshape(shape)
    part = attend_near(span_rank, near, q_rows)
    out = attend_far(span_rank, levels, head, near, far, *part, gate_table, q_rows)
    back = lax.all_to_all(out.reshape(spans * senders, q_rows, HD), WIDE, 0, 0, tiled=True)
    return unpack(back, rows)[None]


def solution(mesh):
    fine = Mesh(mesh.devices.reshape(SIZES), AXES)
    split = P(("yh", "z"), ("x", "yl", "c"), None)
    return jax.shard_map(
        local,
        mesh=fine,
        in_specs=(split, split, split, P(), P(), P()),
        out_specs=split,
        check_vma=False,
    )
```

```python
import functools

import jax
import jax.numpy as jnp
from jax import lax
from jax.experimental import pallas as pl
from jax.experimental.pallas import tpu as pltpu
from jax.sharding import Mesh
from jax.sharding import PartitionSpec as P

HD = 128
AXES = ("y1", "z1", "z0", "x1", "x0", "y0", "c")
SPAN_AXES = AXES[:3]
SEQ_AXES = AXES[3:]
WIDE = ("x1", "x0", "y1", "y0", "z1", "z0")
HEAD_AXES = WIDE[:-1]
PARTS = 2
MIB = 1 << 20
VMEM_WHOLE = pl.BlockSpec(memory_space=pltpu.VMEM)
SMEM_WHOLE = pl.BlockSpec(memory_space=pltpu.SMEM)
HBM_WHOLE = pl.BlockSpec(memory_space=pltpu.HBM)
LOG2E = 1.4426950408889634
ROW_BY_ROW = (((1,), (1,)), ((), ()))


def pack_body(q_hbm, k_hbm, v_hbm, o_ref, q_ref, k_ref, v_ref, sems):
    copies = [
        pltpu.make_async_copy(src, dst, sems.at[i])
        for i, (src, dst) in enumerate(((q_hbm, q_ref), (k_hbm, k_ref), (v_hbm, v_ref)))
    ]
    for copy in copies:
        copy.start()
    rows, width = q_ref.shape
    heads = width // HD
    parts = o_ref.shape[0] // heads
    q_rows = rows // parts
    copies[0].wait()
    for h in range(heads):
        for p in range(parts):
            o_ref[h * parts + p, 0:q_rows, :] = q_ref[
                p * q_rows : (p + 1) * q_rows, h * HD : (h + 1) * HD
            ]
    for n, ref in enumerate((k_ref, v_ref)):
        copies[n + 1].wait()
        for h in range(heads):
            block = ref[:, h * HD : (h + 1) * HD]
            for p in range(parts):
                o_ref[h * parts + p, q_rows + n * rows : q_rows + (n + 1) * rows, :] = block


def pack(q, k, v, parts):
    rows, width = q.shape
    return pl.pallas_call(
        pack_body,
        out_shape=jax.ShapeDtypeStruct(
            (width // HD * parts, rows // parts + 2 * rows, HD), q.dtype
        ),
        in_specs=[HBM_WHOLE] * 3,
        out_specs=VMEM_WHOLE,
        scratch_shapes=[pltpu.VMEM((rows, width), q.dtype)] * 3
        + [pltpu.SemaphoreType.DMA((3,))],
        compiler_params=pltpu.CompilerParams(vmem_limit_bytes=6 * MIB),
        name="pack",
    )(*(pltpu.with_memory_space_constraint(a, pltpu.HBM) for a in (q, k, v)))


def sent_by(span):
    bits = len(SPAN_AXES)
    return tuple(
        (span >> (bits - 1 - SPAN_AXES.index(axis))) & 1 if axis in SPAN_AXES else slice(None)
        for axis in WIDE
    )


def span_order(rank, spans):
    order = []
    for place in range(spans):
        span = jnp.int32(0)
        for s in range(1, spans):
            span = jnp.where(rank[s] == place, s, span)
        order.append(span)
    return order


def take(ref, span, start, stop):
    hd = ref.shape[-1]
    block = ref[sent_by(span) + (slice(start, stop), slice(None))]
    return block.reshape(block.size // hd, hd)


def sizes(rank, ref):
    spans = rank.shape[0]
    senders = 2 ** len(WIDE) // spans
    return spans, senders, ref.shape[-2], ref.shape[-1]


def score_visible(order, shape, q_ref, kv_ref, q_rows, q_s, s_s):
    spans, senders, packed, hd = shape
    rows = (packed - q_rows) // 2
    q_step, k_step = senders * q_rows, senders * rows
    for r in range(spans):
        q_s[r * q_step : (r + 1) * q_step, :] = take(q_ref, order[r], 0, q_rows)
    for b in range(spans):
        k = take(kv_ref, order[b], q_rows, q_rows + rows)
        s_s[b * q_step :, b * k_step : (b + 1) * k_step] = lax.dot_general(
            q_s[b * q_step :, :], k, ROW_BY_ROW, preferred_element_type=jnp.float32
        )


def weighted_values(order, shape, g, group, kv_ref, q_rows, p_s):
    spans, senders, packed, hd = shape
    rows = (packed - q_rows) // 2
    q_step, k_step = senders * q_rows, senders * rows
    for a in range(group - 1):
        r = g * group + a
        p_s[r * q_step : (r + 1) * q_step, (r + 1) * k_step : (g + 1) * group * k_step] = jnp.zeros(
            (q_step, (group - 1 - a) * k_step), p_s.dtype
        )
    acc = None
    for b in range((g + 1) * group):
        v = take(kv_ref, order[b], q_rows + rows, packed)
        part = jnp.dot(
            p_s[g * group * q_step : (g + 1) * group * q_step, b * k_step : (b + 1) * k_step],
            v,
            preferred_element_type=jnp.float32,
        )
        acc = part if acc is None else acc + part
    return acc


def near_body(q_rows, rank, near_ref, acc_ref, top_ref, total_ref, q_s, s_s, p_s):
    shape = spans, senders, packed, hd = sizes(rank, near_ref)
    q_step, k_step = senders * q_rows, senders * (packed - q_rows) // 2
    factor = LOG2E / hd**0.5
    order = span_order(rank, spans)
    score_visible(order, shape, near_ref, near_ref, q_rows, q_s, s_s)
    for r in range(spans):
        here = slice(r * q_step, (r + 1) * q_step)
        s = s_s[here, 0 : (r + 1) * k_step]
        top = jnp.max(s, axis=1, keepdims=True)
        e = jnp.exp2((s - top) * factor)
        top_ref[here, :] = top
        total_ref[here, :] = jnp.sum(e, axis=1, keepdims=True)
        p_s[here, 0 : (r + 1) * k_step] = e.astype(p_s.dtype)
    for g in range(spans // 2):
        acc_ref[2 * g * q_step : 2 * (g + 1) * q_step, :] = weighted_values(
            order, shape, g, 2, near_ref, q_rows, p_s
        )


def far_body(
    q_rows, rank, levels, head, near_ref, far_ref, acc_ref, top_ref, total_ref, gate_ref,
    o_ref, q_s, s_s, p_s, g_s, scale_s, total_s, sem,
):
    shape = spans, senders, packed, hd = sizes(rank, near_ref)
    q_step, k_step = senders * q_rows, senders * (packed - q_rows) // 2
    factor = LOG2E / hd**0.5
    columns = pl.ds(pl.multiple_of(head[0] * hd, hd), hd)
    fetch = pltpu.make_async_copy(gate_ref.at[:, columns], g_s, sem)
    fetch.start()
    order = span_order(rank, spans)
    score_visible(order, shape, near_ref, far_ref, q_rows, q_s, s_s)
    for r in range(spans):
        here = slice(r * q_step, (r + 1) * q_step)
        s = s_s[here, 0 : (r + 1) * k_step]
        top = jnp.maximum(jnp.max(s, axis=1, keepdims=True), top_ref[here, :])
        e = jnp.exp2((s - top) * factor)
        scale = jnp.exp2((top_ref[here, :] - top) * factor)
        scale_s[here, :] = scale
        total_s[here, :] = total_ref[here, :] * scale + jnp.sum(e, axis=1, keepdims=True)
        p_s[here, 0 : (r + 1) * k_step] = e.astype(p_s.dtype)
    fetch.wait()
    for g in range(spans // 2):
        acc = weighted_values(order, shape, g, 2, far_ref, q_rows, p_s)
        for a in range(2):
            r = 2 * g + a
            here = slice(r * q_step, (r + 1) * q_step)
            both = acc_ref[here, :] * scale_s[here, :] + acc[a * q_step : (a + 1) * q_step, :]
            attended = (both / total_s[here, :]).astype(jnp.bfloat16).astype(jnp.float32)
            gated = (g_s[pl.ds(levels[order[r]], 1), :] * attended).astype(o_ref.dtype)
            home = sent_by(order[r])
            free = tuple(2 for at in home if isinstance(at, slice))
            o_ref[home + (slice(None), slice(None))] = gated.reshape(free + (q_rows, hd))


def attend_scratch(spans, senders, q_rows, rows, hd, dtype):
    q_total, k_total = spans * senders * q_rows, spans * senders * rows
    return [
        pltpu.VMEM((q_total, hd), dtype),
        pltpu.VMEM((q_total, k_total), jnp.float32),
        pltpu.VMEM((q_total, k_total), dtype),
    ]


def attend_near(rank, near, q_rows):
    spans, senders, packed, hd = sizes(rank, near)
    rows = (packed - q_rows) // 2
    q_total, k_total = spans * senders * q_rows, spans * senders * rows
    return pl.pallas_call(
        functools.partial(near_body, q_rows),
        out_shape=(
            jax.ShapeDtypeStruct((q_total, hd), jnp.float32),
            jax.ShapeDtypeStruct((q_total, 1), jnp.float32),
            jax.ShapeDtypeStruct((q_total, 1), jnp.float32),
        ),
        in_specs=[SMEM_WHOLE, VMEM_WHOLE],
        out_specs=(VMEM_WHOLE,) * 3,
        scratch_shapes=attend_scratch(spans, senders, q_rows, rows, hd, near.dtype),
        compiler_params=pltpu.CompilerParams(vmem_limit_bytes=24 * MIB),
        cost_estimate=pl.CostEstimate(
            flops=4 * q_total * k_total * hd, bytes_accessed=8 * MIB, transcendentals=0
        ),
        name="attend_near",
    )(rank, near)


def attend_far(rank, levels, head, near, far, acc, top, total, gate_table, q_rows):
    spans, senders, packed, hd = sizes(rank, near)
    rows = (packed - q_rows) // 2
    q_total = spans * senders * q_rows
    return pl.pallas_call(
        functools.partial(far_body, q_rows),
        out_shape=jax.ShapeDtypeStruct(near.shape[:-2] + (q_rows, hd), near.dtype),
        in_specs=[SMEM_WHOLE] * 3 + [VMEM_WHOLE] * 5 + [HBM_WHOLE],
        out_specs=VMEM_WHOLE,
        scratch_shapes=attend_scratch(spans, senders, q_rows, rows, hd, near.dtype)
        + [
            pltpu.VMEM((gate_table.shape[0], hd), gate_table.dtype),
            pltpu.VMEM((q_total, 1), jnp.float32),
            pltpu.VMEM((q_total, 1), jnp.float32),
            pltpu.SemaphoreType.DMA,
        ],
        compiler_params=pltpu.CompilerParams(vmem_limit_bytes=24 * MIB),
        name="attend_far",
    )(rank, levels, head, near, far, acc, top, total, gate_table)


def unpack_body(a_ref, o_ref):
    parts_heads, q_rows, hd = a_ref.shape
    parts = o_ref.shape[0] // q_rows
    for h in range(parts_heads // parts):
        for p in range(parts):
            o_ref[p * q_rows : (p + 1) * q_rows, h * hd : (h + 1) * hd] = a_ref[h * parts + p]


def unpack(a, rows):
    parts_heads, q_rows, hd = a.shape
    return pl.pallas_call(
        unpack_body,
        out_shape=jax.ShapeDtypeStruct((rows, parts_heads * q_rows // rows * hd), a.dtype),
        in_specs=[VMEM_WHOLE],
        out_specs=VMEM_WHOLE,
        compiler_params=pltpu.CompilerParams(vmem_limit_bytes=4 * MIB),
        name="unpack",
    )(a)


def local(queries, keys, values, gate_table, levels, span_rank):
    rows = queries.shape[1]
    q_rows = rows // PARTS
    head = lax.axis_index(HEAD_AXES).astype(jnp.int32).reshape(1)
    packed = pack(queries[0], keys[0], values[0], PARTS)
    near = lax.all_to_all(packed, WIDE, 0, 0, tiled=True)
    far = lax.ppermute(near, "c", [(0, 1), (1, 0)])
    shape = (2,) * len(WIDE) + near.shape[1:]
    near, far = near.reshape(shape), far.reshape(shape)
    part = attend_near(span_rank, near, q_rows)
    out = attend_far(span_rank, levels, head, near, far, *part, gate_table, q_rows)
    back = lax.all_to_all(out.reshape((-1,) + out.shape[-2:]), WIDE, 0, 0, tiled=True)
    return unpack(back, rows)[None]


def solution(mesh):
    fine = Mesh(mesh.devices.reshape((2,) * len(AXES)), AXES)
    split = P(SPAN_AXES, SEQ_AXES, None)
    return jax.shard_map(
        local,
        mesh=fine,
        in_specs=(split, split, split, P(), P(), P()),
        out_specs=split,
        check_vma=False,
    )
```

```python
import functools

import jax
import jax.numpy as jnp
from jax import lax
from jax.experimental import pallas as pl
from jax.experimental.pallas import tpu as pltpu
from jax.sharding import Mesh
from jax.sharding import PartitionSpec as P

HD = 128
AXES = ("y1", "z1", "z0", "x1", "x0", "y0", "c")
SPAN_AXES = AXES[:3]
SEQ_AXES = AXES[3:]
WIDE = ("x1", "x0", "y1", "y0", "z1", "z0")
HEAD_AXES = WIDE[:-1]
PARTS = 2
MIB = 1 << 20
VMEM_WHOLE = pl.BlockSpec(memory_space=pltpu.VMEM)
SMEM_WHOLE = pl.BlockSpec(memory_space=pltpu.SMEM)
HBM_WHOLE = pl.BlockSpec(memory_space=pltpu.HBM)
LOG2E = 1.4426950408889634
ROW_BY_ROW = (((1,), (1,)), ((), ()))


def pack_body(q_hbm, k_hbm, v_hbm, o_ref, q_ref, k_ref, v_ref, sems):
    copies = [
        pltpu.make_async_copy(src, dst, sems.at[i])
        for i, (src, dst) in enumerate(((q_hbm, q_ref), (k_hbm, k_ref), (v_hbm, v_ref)))
    ]
    for copy in copies:
        copy.start()
    rows, width = q_ref.shape
    heads = width // HD
    parts = o_ref.shape[0] // heads
    q_rows = rows // parts
    copies[0].wait()
    for h in range(heads):
        for p in range(parts):
            o_ref[h * parts + p, 0:q_rows, :] = q_ref[
                p * q_rows : (p + 1) * q_rows, h * HD : (h + 1) * HD
            ]
    for n, ref in enumerate((k_ref, v_ref)):
        copies[n + 1].wait()
        for h in range(heads):
            block = ref[:, h * HD : (h + 1) * HD]
            for p in range(parts):
                o_ref[h * parts + p, q_rows + n * rows : q_rows + (n + 1) * rows, :] = block


def pack(q, k, v, parts):
    rows, width = q.shape
    return pl.pallas_call(
        pack_body,
        out_shape=jax.ShapeDtypeStruct(
            (width // HD * parts, rows // parts + 2 * rows, HD), q.dtype
        ),
        in_specs=[HBM_WHOLE] * 3,
        out_specs=VMEM_WHOLE,
        scratch_shapes=[pltpu.VMEM((rows, width), q.dtype)] * 3
        + [pltpu.SemaphoreType.DMA((3,))],
        compiler_params=pltpu.CompilerParams(vmem_limit_bytes=6 * MIB),
        name="pack",
    )(*(pltpu.with_memory_space_constraint(a, pltpu.HBM) for a in (q, k, v)))


def sent_by(span):
    bits = len(SPAN_AXES)
    return tuple(
        (span >> (bits - 1 - SPAN_AXES.index(axis))) & 1 if axis in SPAN_AXES else slice(None)
        for axis in WIDE
    )


def span_order(rank, spans):
    order = []
    for place in range(spans):
        span = jnp.int32(0)
        for s in range(1, spans):
            span = jnp.where(rank[s] == place, s, span)
        order.append(span)
    return order


def take(ref, span, start, stop):
    hd = ref.shape[-1]
    block = ref[sent_by(span) + (slice(start, stop), slice(None))]
    return block.reshape(block.size // hd, hd)


def sizes(rank, ref):
    spans = rank.shape[0]
    senders = 2 ** len(WIDE) // spans
    return spans, senders, ref.shape[-2], ref.shape[-1]


def attend_blocks(order, shape, q_ref, kv_ref, q_rows, s_s, past_top, finish):
    spans, senders, packed, hd = shape
    rows = (packed - q_rows) // 2
    q_step, k_step = senders * q_rows, senders * rows
    factor = LOG2E / hd**0.5
    lanes = [slice(i * hd, (i + 1) * hd) for i in range(k_step // hd)]

    def members(g, b):
        return (0, 1) if b <= 2 * g else (1,)

    def span_rows(which):
        return slice(which[0] * q_step, (which[-1] + 1) * q_step)

    def score(g, b, queries, tops):
        which = members(g, b)
        scores = lax.dot_general(
            queries[span_rows(which), :],
            take(kv_ref, order[b], q_rows, q_rows + rows),
            ROW_BY_ROW,
            preferred_element_type=jnp.float32,
        )
        s_s[g % 2][span_rows(which), b * k_step : (b + 1) * k_step] = scores
        for n, a in enumerate(which):
            for at in lanes:
                part = scores[n * q_step : (n + 1) * q_step, at]
                tops[a] = part if tops[a] is None else jnp.maximum(tops[a], part)

    def weigh(g, b, top, sums):
        which = members(g, b)
        values = take(kv_ref, order[b], q_rows + rows, packed)
        values = jnp.concatenate([values, jnp.ones_like(values)], axis=1)
        weights = []
        for a in which:
            s = s_s[g % 2][span_rows((a,)), b * k_step : (b + 1) * k_step]
            parts = [
                jnp.exp2((s[:, at] - top[a]) * factor).astype(jnp.bfloat16) for at in lanes
            ]
            weights.append(jnp.concatenate(parts, axis=1))
        w = weights[0] if len(weights) == 1 else jnp.concatenate(weights, axis=0)
        part = jnp.dot(w, values, preferred_element_type=jnp.float32)
        for n, a in enumerate(which):
            piece = part[n * q_step : (n + 1) * q_step, :]
            sums[a] = piece if sums[a] is None else sums[a] + piece

    def queries_of(g):
        return jnp.concatenate(
            [take(q_ref, order[2 * g + a], 0, q_rows) for a in range(2)], axis=0
        )

    last = spans // 2 - 1
    queries, tops = queries_of(last), [None, None]
    for b in range(2 * last + 2):
        score(last, b, queries, tops)
    for g in range(last, -1, -1):
        top = []
        for a in range(2):
            most = jnp.broadcast_to(jnp.max(tops[a], axis=1, keepdims=True), tops[a].shape)
            top.append(most if past_top is None else jnp.maximum(most, past_top(2 * g + a)))
        sums, tops = [None, None], [None, None]
        if g > 0:
            queries = queries_of(g - 1)
        for b in range(2 * g + 2):
            if b < 2 * g:
                score(g - 1, b, queries, tops)
            weigh(g, b, top, sums)
        for a in range(2):
            finish(2 * g + a, top[a], sums[a][:, hd:], sums[a][:, 0:hd])


def near_body(q_rows, rank, near_ref, acc_ref, top_ref, total_ref, even_s, odd_s):
    shape = spans, senders, packed, hd = sizes(rank, near_ref)
    q_step = senders * q_rows
    order = span_order(rank, spans)

    def finish(r, top, total, acc):
        here = slice(r * q_step, (r + 1) * q_step)
        acc_ref[here, :] = acc
        top_ref[here, :] = top
        total_ref[here, :] = total

    attend_blocks(order, shape, near_ref, near_ref, q_rows, (even_s, odd_s), None, finish)


def far_body(
    q_rows, rank, levels, head, near_ref, far_ref, acc_ref, top_ref, total_ref, gate_ref,
    o_ref, even_s, odd_s, g_s, sem,
):
    shape = spans, senders, packed, hd = sizes(rank, near_ref)
    q_step = senders * q_rows
    factor = LOG2E / hd**0.5
    columns = pl.ds(pl.multiple_of(head[0] * hd, hd), hd)
    fetch = pltpu.make_async_copy(gate_ref.at[:, columns], g_s, sem)
    fetch.start()
    order = span_order(rank, spans)
    arrived = []

    def past_top(r):
        return top_ref[r * q_step : (r + 1) * q_step, :]

    def finish(r, top, total, acc):
        if not arrived:
            fetch.wait()
            arrived.append(r)
        here = slice(r * q_step, (r + 1) * q_step)
        scale = jnp.exp2((top_ref[here, :] - top) * factor)
        both = acc_ref[here, :] * scale + acc
        attended = both / (total_ref[here, :] * scale + total)
        attended = attended.astype(jnp.bfloat16).astype(jnp.float32)
        gated = (g_s[pl.ds(levels[order[r]], 1), :] * attended).astype(o_ref.dtype)
        home = sent_by(order[r])
        free = tuple(2 for at in home if isinstance(at, slice))
        o_ref[home + (slice(None), slice(None))] = gated.reshape(free + (q_rows, hd))

    attend_blocks(order, shape, near_ref, far_ref, q_rows, (even_s, odd_s), past_top, finish)


def score_scratch(spans, senders, q_rows, rows):
    return [pltpu.VMEM((2 * senders * q_rows, spans * senders * rows), jnp.float32)] * 2


def attend_near(rank, near, q_rows):
    spans, senders, packed, hd = sizes(rank, near)
    rows = (packed - q_rows) // 2
    q_total, k_total = spans * senders * q_rows, spans * senders * rows
    return pl.pallas_call(
        functools.partial(near_body, q_rows),
        out_shape=(
            jax.ShapeDtypeStruct((q_total, hd), jnp.float32),
            jax.ShapeDtypeStruct((q_total, hd), jnp.float32),
            jax.ShapeDtypeStruct((q_total, hd), jnp.float32),
        ),
        in_specs=[SMEM_WHOLE, VMEM_WHOLE],
        out_specs=(VMEM_WHOLE,) * 3,
        scratch_shapes=score_scratch(spans, senders, q_rows, rows),
        compiler_params=pltpu.CompilerParams(vmem_limit_bytes=24 * MIB),
        cost_estimate=pl.CostEstimate(
            flops=4 * q_total * k_total * hd, bytes_accessed=8 * MIB, transcendentals=0
        ),
        name="attend_near",
    )(rank, near)


def attend_far(rank, levels, head, near, far, acc, top, total, gate_table, q_rows):
    spans, senders, packed, hd = sizes(rank, near)
    rows = (packed - q_rows) // 2
    q_total = spans * senders * q_rows
    return pl.pallas_call(
        functools.partial(far_body, q_rows),
        out_shape=jax.ShapeDtypeStruct(near.shape[:-2] + (q_rows, hd), near.dtype),
        in_specs=[SMEM_WHOLE] * 3 + [VMEM_WHOLE] * 5 + [HBM_WHOLE],
        out_specs=VMEM_WHOLE,
        scratch_shapes=score_scratch(spans, senders, q_rows, rows)
        + [
            pltpu.VMEM((gate_table.shape[0], hd), gate_table.dtype),
            pltpu.SemaphoreType.DMA,
        ],
        compiler_params=pltpu.CompilerParams(vmem_limit_bytes=24 * MIB),
        name="attend_far",
    )(rank, levels, head, near, far, acc, top, total, gate_table)


def unpack_body(a_ref, o_ref):
    parts_heads, q_rows, hd = a_ref.shape
    parts = o_ref.shape[0] // q_rows
    for h in range(parts_heads // parts):
        for p in range(parts):
            o_ref[p * q_rows : (p + 1) * q_rows, h * hd : (h + 1) * hd] = a_ref[h * parts + p]


def unpack(a, rows):
    parts_heads, q_rows, hd = a.shape
    return pl.pallas_call(
        unpack_body,
        out_shape=jax.ShapeDtypeStruct((rows, parts_heads * q_rows // rows * hd), a.dtype),
        in_specs=[VMEM_WHOLE],
        out_specs=VMEM_WHOLE,
        compiler_params=pltpu.CompilerParams(vmem_limit_bytes=4 * MIB),
        name="unpack",
    )(a)


def local(queries, keys, values, gate_table, levels, span_rank):
    rows = queries.shape[1]
    q_rows = rows // PARTS
    head = lax.axis_index(HEAD_AXES).astype(jnp.int32).reshape(1)
    packed = pack(queries[0], keys[0], values[0], PARTS)
    near = lax.all_to_all(packed, WIDE, 0, 0, tiled=True)
    far = lax.ppermute(near, "c", [(0, 1), (1, 0)])
    shape = (2,) * len(WIDE) + near.shape[1:]
    near, far = near.reshape(shape), far.reshape(shape)
    part = attend_near(span_rank, near, q_rows)
    out = attend_far(span_rank, levels, head, near, far, *part, gate_table, q_rows)
    back = lax.all_to_all(out.reshape((-1,) + out.shape[-2:]), WIDE, 0, 0, tiled=True)
    return unpack(back, rows)[None]


def solution(mesh):
    fine = Mesh(mesh.devices.reshape((2,) * len(AXES)), AXES)
    split = P(SPAN_AXES, SEQ_AXES, None)
    return jax.shard_map(
        local,
        mesh=fine,
        in_specs=(split, split, split, P(), P(), P()),
        out_specs=split,
        check_vma=False,
    )
```
